256 devices in a mesh: passage: 32 (over x, z_hi, core), span: 8 (over z_lo, y).
Axes of the slice: x: 4, y: 4, z: 8 (z_hi: 4, z_lo: 2; z = z_hi * 2 + z_lo), core: 2. Of those that a mesh axis runs over, the one named last changes fastest.
Arguments:
- state: float32 [7, 32, 48, 128, 128], P(None, 'passage', None, 'span'), may hold values from -6 to 6
- previous: float32 [7, 32, 48, 128, 128], P(None, 'passage', None, 'span'), may hold values from -6 to 6
- earlier: float32 [7, 32, 48, 128, 128], P(None, 'passage', None, 'span'), may hold values from -6 to 6
- axial_speed: float32 [32, 48, 128, 128], P('passage', None, 'span'), may hold values from 0.2 to 1
- pitch_speed: float32 [32, 48, 128, 128], P('passage', None, 'span'), may hold values from -0.6 to 0.6
- viscosity: float32 [32, 48, 128, 128], P('passage', None, 'span'), may hold values from 0.02 to 0.2
- inflow: float32 [7, 128, 128], P(None, 'span'), may hold values from -6 to 6
- coupling: float32 [7, 7], replicated, may hold values from -2 to 2
- partner: int32 [32], replicated, may hold values from 0 to 31, as said below
- tile_ids: int32 [32, 8, 4], replicated, may hold values from 0 to 255, as said below
- tile_weights: int32 [32, 8, 4], replicated, may hold values from 1 to 16
Outputs:
- updated: float32 [7, 32, 48, 128, 128], P(None, 'passage', None, 'span')
The draws below stay inside these ranges and needn't reach their ends.
Inputs may be any that keep to these rules, and one draw needn't show every extreme that they name: `partner`: rotor passages' partners form one cycle through all rotor passages, stator passages' partners one cycle through all stator passages; each cycle gives its row's order around the annulus. `tile_ids`: A rotor passage's tiles list tiles of stator passages and a stator passage's tiles list tiles of rotor passages; each list names 4 consecutive tiles of the other row, taken in that row's annulus order (its partner cycle, tiles of a passage in order), cyclically; every tile is named by exactly 4 lists, and tile a lists tile b exactly when b lists a.
All inputs are finite; a program needn't handle non-finite values.
Results may differ from the reference program's by a relative error of at most 0.00005.
Values sent between devices are 32-bit elements; how exact they have to be, the bound alone decides.
No kernel may reach another device: no remote copies, remote signals or barrier semaphores. Data moves between devices by JAX's collectives and lax.ppermute only.
A program may use at most 128 MiB of HBM per device.

```python
import math
import jax
import jax.numpy as jnp
from jax import lax

FIELDS = 7
AX = 48
PITCH = 128
TPP = 8
INTERSECTION = 4
PASSAGES = 32
SPAN = 128


def annulus_orders(key):
    count = PASSAGES
    half = count // 2
    passage_ids = jnp.arange(count, dtype=jnp.int32)
    rotor = (passage_ids + (passage_ids >= half).astype(jnp.int32)) % 4 < 2
    keys = jax.random.split(key, 5)
    first_pair = 4 * jax.random.randint(keys[0], (), 0, count // 8, dtype=jnp.int32)
    second_pair = 4 * jax.random.randint(keys[1], (), 0, count // 8, dtype=jnp.int32) + 1
    ranks = 2 * jax.random.permutation(keys[2], count).astype(jnp.int32)
    ranks = ranks.at[first_pair + half].set(ranks[first_pair] + 1)
    ranks = ranks.at[second_pair + 1].set(ranks[second_pair + half] + 1)
    large_key = 4 * count
    rotor_order = jnp.argsort(jnp.where(rotor, ranks, large_key), stable=True)[:half].astype(jnp.int32)
    stator_base = jnp.argsort(jnp.where(rotor, large_key, ranks), stable=True)[:half].astype(jnp.int32)
    coarse = jax.random.randint(keys[3], (), 0, half, dtype=jnp.int32)
    fine = jax.random.randint(keys[4], (), 0, TPP, dtype=jnp.int32)
    place = jnp.argmax(rotor_order == second_pair).astype(jnp.int32)
    base_at = jnp.argmax(stator_base == second_pair + half).astype(jnp.int32)
    positions = jnp.arange(half, dtype=jnp.int32)
    stator_order = stator_base[(positions - place - coarse + base_at) % half]
    return (rotor_order, stator_order, coarse * TPP + fine)


def draw_partner(key, part):
    rotor_order, stator_order, angle = annulus_orders(key)
    table = jnp.zeros((PASSAGES,), jnp.int32)
    table = table.at[rotor_order].set(jnp.roll(rotor_order, -1))
    table = table.at[stator_order].set(jnp.roll(stator_order, -1))
    return table


def draw_tile_ids(key, part):
    rotor_order, stator_order, angle = annulus_orders(key)
    half = PASSAGES // 2
    row_tiles = half * TPP
    positions = jnp.zeros((PASSAGES,), jnp.int32)
    positions = positions.at[rotor_order].set(jnp.arange(half, dtype=jnp.int32))
    positions = positions.at[stator_order].set(jnp.arange(half, dtype=jnp.int32))
    passage_ids = jnp.arange(PASSAGES, dtype=jnp.int32)
    rotor = ((passage_ids + (passage_ids >= half).astype(jnp.int32)) % 4 < 2)[:, None, None]
    tile_index = jnp.arange(TPP, dtype=jnp.int32)[None, :, None]
    member = jnp.arange(INTERSECTION, dtype=jnp.int32)[None, None, :]
    within = positions[:, None, None] * TPP + tile_index
    toward_stator = (within + angle + member) % row_tiles
    toward_rotor = (within - angle - INTERSECTION + 1 + member) % row_tiles
    stator_tiles = stator_order[toward_stator // TPP] * TPP + toward_stator % TPP
    rotor_tiles = rotor_order[toward_rotor // TPP] * TPP + toward_rotor % TPP
    return jnp.where(rotor, stator_tiles, rotor_tiles).astype(jnp.int32)


def with_ends(entries, rng, low, largest):
    longest = entries.shape.index(max(entries.shape))
    spots = []
    for shift in (0, 1):
        where = [jax.random.randint(jax.random.fold_in(rng, axis), (), 0, length) for axis, length in enumerate(entries.shape)]
        where[longest] = (where[longest] + shift) % entries.shape[longest]
        spots.append(tuple(where))
    return entries.at[spots[0]].set(low).at[spots[1]].set(largest)


def block_scale(rng, dims, cuts, low, high):
    loudness, own = 1.0, jax.random.fold_in(rng, 6)
    for position, parts in cuts:
        heights = jnp.exp(jax.random.uniform(jax.random.fold_in(own, position), (parts,), jnp.float32, low / len(cuts), high / len(cuts)))
        loudness = loudness * jnp.repeat(heights, dims[position] // parts).reshape([-1 if axis == position else 1 for axis in range(len(dims))])
    return loudness


def bell_draw(key, extent, scale, bound, pieces=(), kind=jnp.bfloat16):
    values = jax.random.normal(key, extent, jnp.float32) * scale
    if len(pieces) > 0:
        values = block_scale(key, extent, pieces, -0.22, 0.18) * values
    return jnp.clip(values, min=-bound, max=bound).astype(kind)


def setup_inputs(seed: int = 0) -> dict:
    seeds = jax.random.split(jax.random.key(seed), 12)
    state = bell_draw(seeds[0], (FIELDS, PASSAGES, AX, SPAN, PITCH), 1.0, 6.0, ((1, 32), (3, 8)), jnp.float32)
    previous = bell_draw(seeds[1], (FIELDS, PASSAGES, AX, SPAN, PITCH), 1.0, 6.0, ((1, 32), (3, 8)), jnp.float32)
    earlier = bell_draw(seeds[2], (FIELDS, PASSAGES, AX, SPAN, PITCH), 1.0, 6.0, ((1, 32), (3, 8)), jnp.float32)
    axial_speed = jnp.clip(jnp.exp(math.log(1.0) - 1.609438 * jax.random.uniform(seeds[3], (PASSAGES, AX, SPAN, PITCH), jnp.float32) ** block_scale(seeds[3], (PASSAGES, AX, SPAN, PITCH), ((0, 32), (2, 8)), -0.2, 0.2)), 0.2, 1.0)
    pitch_speed = jnp.clip(jax.random.uniform(seeds[4], (PASSAGES, AX, SPAN, PITCH), jnp.float32, -0.6, 0.6) * block_scale(seeds[4], (PASSAGES, AX, SPAN, PITCH), ((0, 32), (2, 8)), -0.4, 0.0), -0.6, 0.6)
    viscosity = jnp.clip(jnp.exp(math.log(0.2) - 2.3025851 * jax.random.uniform(seeds[5], (PASSAGES, AX, SPAN, PITCH), jnp.float32) ** block_scale(seeds[5], (PASSAGES, AX, SPAN, PITCH), ((0, 32), (2, 8)), -0.2, 0.2)), 0.02, 0.2)
    inflow = bell_draw(seeds[6], (FIELDS, SPAN, PITCH), 1.0, 6.0, ((1, 8),), jnp.float32)
    coupling = bell_draw(seeds[7], (FIELDS, FIELDS), FIELDS ** -0.5, 2.0, (), jnp.float32)
    partner = draw_partner(jax.random.fold_in(seeds[11], 71), 0)
    tile_ids = draw_tile_ids(jax.random.fold_in(seeds[11], 71), 0)
    tile_weights = with_ends(jax.random.randint(seeds[10], (PASSAGES, TPP, INTERSECTION), 1, 17), jax.random.fold_in(seeds[10], 1), 1, 16).astype(jnp.int32)
    return {"state": state, "previous": previous, "earlier": earlier, "axial_speed": axial_speed, "pitch_speed": pitch_speed, "viscosity": viscosity, "inflow": inflow, "coupling": coupling, "partner": partner, "tile_ids": tile_ids, "tile_weights": tile_weights}


CFL = 0.8
STEP_DT = 2.0
FIRST = 0.5
SECOND = 1.0
HIGHEST = lax.Precision.HIGHEST


def residual(current, inlet_ghost, outlet_ghost, below_ghost, above_ghost, spanned, prior, older, speed_axial, speed_pitch, diffusion, coupling):
    axial_line = jnp.concatenate([inlet_ghost[:, None], current, outlet_ghost[:, None]], axis=1)
    pitch_line = jnp.concatenate([below_ghost[..., None], current, above_ghost[..., None]], axis=3)
    forward_axial = axial_line[:, 2:]
    backward_axial = axial_line[:, :-2]
    forward_pitch = pitch_line[..., 2:]
    backward_pitch = pitch_line[..., :-2]
    doubled = 2.0 * current
    spread = (forward_axial - doubled + backward_axial) + (forward_pitch - doubled + backward_pitch) + (spanned[:, :, 2:] - doubled + spanned[:, :, :-2])
    transport = 0.5 * speed_axial * (forward_axial - backward_axial) + 0.5 * speed_pitch * (forward_pitch - backward_pitch)
    mixing = jnp.einsum("fg,gasp->fasp", coupling, current, precision=HIGHEST)
    unsteady = (3.0 * current - 4.0 * prior + older) / (2.0 * STEP_DT)
    return unsteady + transport - diffusion * spread + mixing


def weighted_tiles(faces, tile_ids, tile_weights):
    fields, passages, span_cells, pitch_cells = faces.shape
    tiles_per = tile_ids.shape[1]
    width = pitch_cells // tiles_per
    tiles = faces.reshape(fields, passages, span_cells, tiles_per, width).transpose(0, 1, 3, 2, 4).reshape(fields, passages * tiles_per, span_cells, width)
    weights = tile_weights.astype(jnp.float32)
    shares = weights / jnp.sum(weights, axis=2, keepdims=True)
    columns = jnp.arange(passages * tiles_per, dtype=jnp.int32)
    selected = (tile_ids[:, :, :, None] == columns).astype(jnp.float32)
    matrix = jnp.sum(shares[:, :, :, None] * selected, axis=2).reshape(passages * tiles_per, passages * tiles_per)
    ghost = jnp.einsum("rc,fcsv->frsv", matrix, tiles, precision=HIGHEST)
    return ghost.reshape(fields, passages, tiles_per, span_cells, width).transpose(0, 1, 3, 2, 4).reshape(fields, passages, span_cells, pitch_cells)


def rotor_mask(index_values, passages):
    shifted = index_values + (index_values >= passages // 2).astype(jnp.int32)
    return (shifted % 4) < 2


def reference(state, previous, earlier, axial_speed, pitch_speed, viscosity, inflow, coupling, partner, tile_ids, tile_weights):
    fields, passages, axial_cells, span_cells, pitch_cells = state.shape
    rotor_rows = rotor_mask(jnp.arange(passages, dtype=jnp.int32), passages)[None, :, None, None]
    inverse = jnp.zeros((passages,), jnp.int32).at[partner].set(jnp.arange(passages, dtype=jnp.int32))
    pseudo_dt = CFL / (axial_speed + jnp.abs(pitch_speed) + 6.0 * viscosity + 1.5 / STEP_DT)

    def advance(current, factor):
        faces = jnp.where(rotor_rows, current[:, :, -1], current[:, :, 0])
        sliding = weighted_tiles(faces, tile_ids, tile_weights)
        inlets = jnp.where(rotor_rows, inflow[:, None], sliding)
        outlets = jnp.where(rotor_rows, sliding, current[:, :, -1])
        above_all = current[..., 0][:, partner]
        below_all = current[..., -1][:, inverse]

        def one_passage(passage_id):
            def take_row(array):
                return lax.dynamic_index_in_dim(array, passage_id, 1, keepdims=False)

            def take_first(array):
                return lax.dynamic_index_in_dim(array, passage_id, 0, keepdims=False)

            cells = take_row(current)
            spanned = jnp.pad(cells, ((0, 0), (0, 0), (1, 1), (0, 0)))
            change = residual(cells, take_row(inlets), take_row(outlets), take_row(below_all), take_row(above_all), spanned, take_row(previous), take_row(earlier), take_first(axial_speed), take_first(pitch_speed), take_first(viscosity), coupling)
            return cells - factor * take_first(pseudo_dt) * change

        moved = lax.map(one_passage, jnp.arange(passages, dtype=jnp.int32))
        return jnp.moveaxis(moved, 0, 1)

    middle = advance(state, FIRST)
    return advance(middle, SECOND)
```

```python
import functools

import jax
import jax.numpy as jnp
from jax import lax
from jax.experimental import pallas as pl
from jax.experimental.pallas import tpu as pltpu
from jax.sharding import PartitionSpec as P

CFL = 0.8
STEP_DT = 2.0

X_FLIPS = (8, 16, 24)
Z_FLIPS = (2, 4, 6)
CORE_FLIP = 1
SOURCES = (0, 8, 16, 24, 1, 9, 17, 25)
DESTS = (0, 2, 4, 6)

LAYERS = 8

SMEM = pl.BlockSpec(memory_space=pltpu.SMEM)
VMEM = pl.BlockSpec(memory_space=pltpu.VMEM)


def params():
    return pltpu.CompilerParams(vmem_limit_bytes=48 * 1024 * 1024)


def lanes(shape):
    return lax.broadcasted_iota(jnp.int32, shape, len(shape) - 1)


def pack_kernel(info, s_ref, packet_ref, low_ref, high_ref):
    fields, rows, width = s_ref.shape
    depth = rows // 16
    pair = lanes((8, width)) >> 1
    start = info[1] * (rows - 16)

    def one(f, _):
        packet_ref[f, 0:16, :] = s_ref[f, pl.ds(pl.multiple_of(start, 16), 16), :]
        for h in range(2):
            held = jnp.zeros((8, width), jnp.float32)
            for a in range(depth):
                row = a * 16 + h * 8
                held = jnp.where(
                    pair == a, pltpu.roll(s_ref[f, row : row + 8, :], 2 * a + 1, 1), held
                )
            packet_ref[f, 16 + 8 * h : 24 + 8 * h, :] = held
        low_ref[f] = s_ref[f, pl.ds(0, depth, stride=16), :]
        high_ref[f] = s_ref[f, pl.ds(15, depth, stride=16), :]
        return 0

    lax.fori_loop(0, fields, one, 0)


def pack(info, state):
    fields, rows, width = state.shape
    row = jax.ShapeDtypeStruct((fields, rows // 16, width), jnp.float32)
    return pl.pallas_call(
        pack_kernel,
        out_shape=(jax.ShapeDtypeStruct((fields, 32, width), jnp.float32), row, row),
        in_specs=[SMEM, VMEM],
        out_specs=(VMEM, VMEM, VMEM),
        compiler_params=params(),
        name="pack",
    )(info, state)


def relay_kernel(info, partner, ids_ref, shares_ref, *refs):
    packets, outs, table = refs[:8], refs[8:12], refs[12]
    fields, _, width = packets[0].shape
    own = info[0]
    sources = [own ^ k for k in SOURCES]
    dests = [own ^ k for k in DESTS]
    lane = lanes((8, width))
    turn = lax.broadcasted_iota(jnp.int32, (8, width), 0)
    tile = ((lane >> 4) - turn) & 7
    for d, dest in enumerate(dests):
        wanted = ids_ref[dest]
        share = shares_ref[dest]
        for q, source in enumerate(sources):
            there = tile + source * 8
            total = jnp.zeros((8, width), jnp.float32)
            for k in range(4):
                total = total + jnp.where(wanted[k : k + 1] == there, share[k : k + 1], 0.0)
            table[d, q] = total
    even = (lane & 1) == 0
    above = [[(partner[d] == q).astype(jnp.float32) for q in sources] for d in dests]
    below = [[(partner[q] == d).astype(jnp.float32) for q in sources] for d in dests]

    def one(i, _):
        f = i >> 1
        low = pl.multiple_of((i & 1) * 8, 8)
        high = pl.multiple_of(16 + (i & 1) * 8, 8)
        totals = [jnp.zeros((8, width), jnp.float32) for _ in dests]
        uppers = [jnp.zeros((8, width), jnp.float32) for _ in dests]
        lowers = [jnp.zeros((8, width), jnp.float32) for _ in dests]
        for q in range(8):
            face = packets[q][f, pl.ds(low, 8), :]
            edge = packets[q][f, pl.ds(high, 8), :]
            for t in range(8):
                turned = face if t == 0 else pltpu.roll(face, 16 * t, 1)
                for d in range(4):
                    totals[d] = totals[d] + turned * table[d, q, t : t + 1, :]
            for d in range(4):
                uppers[d] = uppers[d] + above[d][q] * edge
                lowers[d] = lowers[d] + below[d][q] * edge
        for d in range(4):
            outs[d][f, pl.ds(low, 8), :] = totals[d]
            outs[d][f, pl.ds(high, 8), :] = jnp.where(
                even, pltpu.roll(uppers[d], width - 1, 1), pltpu.roll(lowers[d], 1, 1)
            )
        return 0

    lax.fori_loop(0, fields * 2, one, 0)


def relay(info, partner, ids, shares, packets):
    shape = jax.ShapeDtypeStruct(packets[0].shape, jnp.float32)
    return pl.pallas_call(
        relay_kernel,
        out_shape=(shape,) * 4,
        in_specs=[SMEM, SMEM] + [VMEM] * 10,
        out_specs=(VMEM,) * 4,
        scratch_shapes=[pltpu.VMEM((4, 8, 8, 128), jnp.float32)],
        compiler_params=params(),
        name="relay",
    )(info, partner, ids, shares, *packets)


def stage_kernel(first, *refs):
    if first:
        (info, coupling, v_hbm, prior, older, axial, pitch, visc, inflow, halo_low, halo_high) = refs[:11]
        parts, (out, base, packet, low, high), (line, ghost, sem) = refs[11:15], refs[15:20], refs[20:]
    else:
        (info, coupling, v_hbm, base, axial, pitch, visc, inflow, halo_low, halo_high) = refs[:10]
        parts, (out,), (line, ghost, sem) = refs[10:14], refs[14:15], refs[15:]
    fields, rows, width = line.shape[0], line.shape[1] - 32, line.shape[2]
    depth = rows // 16
    step = pl.program_id(0)
    rotor = info[1] == 1

    @pl.when(step == 0)
    def _():
        copy = pltpu.make_async_copy(v_hbm, line.at[:, pl.ds(16, rows), :], sem)
        copy.start()
        for f in range(fields):
            ghost[f] = (parts[0][f] + parts[1][f]) + (parts[2][f] + parts[3][f])
        if first:
            packet[...] = jnp.zeros_like(packet)
        copy.wait()
        for f in range(fields):
            line[f, 0:16, :] = jnp.where(rotor, inflow[f], ghost[f, 0:16, :])
            line[f, rows + 16 : rows + 32, :] = jnp.where(
                rotor, ghost[f, 0:16, :], line[f, rows : rows + 16, :]
            )

    lane = lanes((8, width))
    sub = lax.broadcasted_iota(jnp.int32, (8, width), 0)
    head, tail = lane == 0, lane == width - 1
    top, bottom = sub == 0, sub == 7

    def one(j, _):
        a = step * LAYERS + j
        here = (a + 1) * 16
        back = lax.rem(width - 1 - 2 * a, width)
        coefs = []
        for h in range(2):
            speed = axial[j, 8 * h : 8 * h + 8, :]
            cross = pitch[j, 8 * h : 8 * h + 8, :]
            nu = visc[j, 8 * h : 8 * h + 8, :]
            dt = CFL / (speed + jnp.abs(cross) + 6.0 * nu + 1.5 / STEP_DT)
            spread = dt * nu
            half_axial = 0.5 * dt * speed
            half_pitch = 0.5 * dt * cross
            coefs.append(
                (
                    dt,
                    -(1.5 / STEP_DT) * dt - 6.0 * spread,
                    spread - half_axial,
                    spread + half_axial,
                    spread - half_pitch,
                    spread + half_pitch,
                    spread,
                )
            )

        def at(f, h, shift=0):
            return line[f, pl.ds(pl.multiple_of(here + 16 * shift + 8 * h, 8), 8), :]

        values = [[at(f, h) for h in range(2)] for f in range(fields)]
        for f in range(fields):
            x0, x1 = values[f]
            r0, r1 = pltpu.roll(x0, 1, 0), pltpu.roll(x1, 1, 0)
            d0, d1 = pltpu.roll(x0, 7, 0), pltpu.roll(x1, 7, 0)
            before = (jnp.where(top, halo_low[f, pl.ds(a, 1), :], r0), jnp.where(top, r0, r1))
            after = (jnp.where(bottom, d1, d0), jnp.where(bottom, halo_high[f, pl.ds(a, 1), :], d1))
            for h in range(2):
                dt, centre, forward, backward, right, left, spread = coefs[h]
                x = values[f][h]
                edge = pltpu.roll(ghost[f, 16 + 8 * h : 24 + 8 * h, :], back, 1)
                lower = jnp.where(head, edge, pltpu.roll(x, 1, 1))
                upper = jnp.where(tail, edge, pltpu.roll(x, width - 1, 1))
                mixed = coupling[f, 0] * values[0][h]
                for g in range(1, fields):
                    mixed = mixed + coupling[f, g] * values[g][h]
                change = (
                    (centre * x + spread * (before[h] + after[h]))
                    + (forward * at(f, h, 1) + backward * at(f, h, -1))
                    + (right * upper + left * lower)
                    - dt * mixed
                )
                place = (f, j, slice(8 * h, 8 * h + 8))
                if first:
                    known = dt * (prior[place] - 0.25 * older[place])
                    base[place] = known
                    moved = x + 0.5 * (known + change)
                    out[place] = moved
                    spot = (f, slice(16 + 8 * h, 24 + 8 * h))
                    packet[spot] = jnp.where(
                        (lane >> 1) == a, pltpu.roll(moved, 2 * a + 1, 1), packet[spot]
                    )
                    if h == 0:
                        low[f, pl.ds(j, 1), :] = moved[0:1]
                    else:
                        high[f, pl.ds(j, 1), :] = moved[7:8]
                else:
                    out[place] = x + (base[place] + change)
        return 0

    lax.fori_loop(0, LAYERS, one, 0)

    if first:
        face = info[1] * (depth - 1)

        @pl.when(step == face // LAYERS)
        def _():
            for f in range(fields):
                packet[f, 0:16, :] = out[f, lax.rem(face, LAYERS)]


def stage(first, info, coupling, v, given, speeds, inflow, halos, parts):
    fields, rows, width = v.shape
    depth = rows // 16
    whole = jax.ShapeDtypeStruct((fields, depth, 16, width), jnp.float32)
    block = pl.BlockSpec((fields, LAYERS, 16, width), lambda i: (0, i, 0, 0))
    cell = pl.BlockSpec((LAYERS, 16, width), lambda i: (i, 0, 0))
    line = pl.BlockSpec((fields, LAYERS, width), lambda i: (0, i, 0))
    packet_shape = parts[0].shape

    def fixed(shape):
        return pl.BlockSpec(shape, lambda i: (0,) * len(shape))

    packet = fixed(packet_shape)
    halo = fixed(halos[0].shape)
    out_shape, out_specs = [whole], [block]
    if first:
        edge = jax.ShapeDtypeStruct((fields, depth, width), jnp.float32)
        out_shape += [whole, jax.ShapeDtypeStruct(packet_shape, jnp.float32), edge, edge]
        out_specs += [block, packet, line, line]
    return pl.pallas_call(
        functools.partial(stage_kernel, first),
        grid=(depth // LAYERS,),
        out_shape=out_shape,
        in_specs=[SMEM, SMEM, pl.BlockSpec(memory_space=pl.ANY)]
        + [block] * len(given)
        + [cell] * 3
        + [fixed(inflow.shape), halo, halo]
        + [packet] * 4,
        out_specs=out_specs,
        scratch_shapes=[
            pltpu.VMEM((fields, rows + 32, width), jnp.float32),
            pltpu.VMEM(packet_shape, jnp.float32),
            pltpu.SemaphoreType.DMA(()),
        ],
        compiler_params=params(),
        name="first_stage" if first else "second_stage",
    )(info, coupling, v, *given, *speeds, inflow, *halos, *parts)


def flip(value, bits):
    return lax.ppermute(value, "passage", [(i, i ^ bits) for i in range(lax.axis_size("passage"))])


def spread(low, high):
    count = lax.axis_size("span")
    up = [(i, i + 1) for i in range(count - 1)]
    down = [(i + 1, i) for i in range(count - 1)]
    return lax.ppermute(high, "span", up), lax.ppermute(low, "span", down)


def on_device(
    state,
    previous,
    earlier,
    axial_speed,
    pitch_speed,
    viscosity,
    inflow,
    coupling,
    partner,
    tile_ids,
    tile_weights,
):
    own = lax.axis_index("passage")
    half = lax.axis_size("passage") // 2
    rotor = (own + (own >= half).astype(jnp.int32)) % 4 < 2
    info = jnp.stack([own, rotor.astype(jnp.int32)])
    fields, _, depth, spans, width = state.shape
    cells = state.reshape(fields, depth * spans, width)
    speeds = (axial_speed[0], pitch_speed[0], viscosity[0])
    weights = tile_weights.astype(jnp.float32)
    shares = weights / jnp.sum(weights, axis=2, keepdims=True)
    cut = width // tile_ids.shape[1]
    wide_ids = jnp.repeat(jnp.swapaxes(tile_ids, 1, 2), cut, axis=2)
    wide_shares = jnp.repeat(jnp.swapaxes(shares, 1, 2), cut, axis=2)

    def exchange(packet):
        near = [packet] + [flip(packet, k) for k in X_FLIPS]
        far = [flip(p, CORE_FLIP) for p in near]
        sent = relay(info, partner, wide_ids, wide_shares, near + far)
        return [sent[0]] + [flip(p, k) for p, k in zip(sent[1:], Z_FLIPS)]

    packet, low, high = pack(info, cells)
    parts = exchange(packet)
    halos = spread(low, high)
    middle, base, packet, low, high = stage(
        True, info, coupling, cells, (previous[:, 0], earlier[:, 0]), speeds, inflow, halos, parts
    )
    parts = exchange(packet)
    halos = spread(low, high)
    (updated,) = stage(
        False, info, coupling, middle.reshape(cells.shape), (base,), speeds, inflow, halos, parts
    )
    return updated[:, None]


def solution(mesh):
    placed = (
        P(None, "passage", None, "span", None),
        P(None, "passage", None, "span", None),
        P(None, "passage", None, "span", None),
        P("passage", None, "span", None),
        P("passage", None, "span", None),
        P("passage", None, "span", None),
        P(None, "span", None),
        P(),
        P(),
        P(),
        P(),
    )
    return jax.shard_map(
        on_device,
        mesh=mesh,
        in_specs=placed,
        out_specs=P(None, "passage", None, "span", None),
        check_vma=False,
    )
```

```python
import functools

import jax
import jax.numpy as jnp
from jax import lax
from jax.experimental import pallas as pl
from jax.experimental.pallas import tpu as pltpu
from jax.sharding import PartitionSpec as P

CFL = 0.8
STEP_DT = 2.0

X_FLIPS = (8, 16, 24)
Z_FLIPS = (2, 4, 6)
CORE_FLIP = 1
SOURCES = (0, 8, 16, 24, 1, 9, 17, 25)

LAYERS = 8
UNITS = 14
EDGE = UNITS * 8
DEPTH = 48
TIGHT = 11

SMEM = pl.BlockSpec(memory_space=pltpu.SMEM)
VMEM = pl.BlockSpec(memory_space=pltpu.VMEM)
ANY = pl.BlockSpec(memory_space=pl.ANY)


def params(mib):
    return pltpu.CompilerParams(vmem_limit_bytes=mib * 1024 * 1024)


def lanes(shape=(8, 128)):
    return lax.broadcasted_iota(jnp.int32, shape, len(shape) - 1)


def struct(*shape):
    return jax.ShapeDtypeStruct(shape, jnp.float32)


def fixed(*shape):
    return pl.BlockSpec(shape, lambda i: (0,) * len(shape))


def unit(ref, u):
    return ref[8 * u : 8 * u + 8, :]


def tighten(units):
    lane = lanes()
    packed = []
    for first in range(0, 12, 4):
        for j in range(3):
            spare = pltpu.roll(units[first + 3], 96 - 32 * j, 1)
            packed.append(jnp.where(lane < 96, units[first + j], spare))
    return packed + list(units[12:])


def loosen(packed):
    lane = lanes()
    units = []
    for first in range(0, 9, 3):
        a, b, c = packed[first : first + 3]
        last = jnp.where(
            lane < 32,
            pltpu.roll(a, 32, 1),
            jnp.where(lane < 64, pltpu.roll(b, 64, 1), pltpu.roll(c, 96, 1)),
        )
        units += [a, b, c, last]
    return units + list(packed[9:])


def is_rotor(passage):
    return ((passage + (passage >= 16).astype(jnp.int32)) & 3) < 2


def summed(parts, u):
    return (unit(parts[0], u) + unit(parts[1], u)) + (unit(parts[2], u) + unit(parts[3], u))


def chunk_copy(source, target, sem, c, base=0):
    rows = LAYERS * 16
    here = pl.multiple_of(c * rows, rows)
    there = pl.multiple_of(here + base, 16)
    return pltpu.make_async_copy(
        source.at[:, pl.ds(here, rows), :], target.at[:, pl.ds(there, rows), :], sem.at[c]
    )


def add_terms(info, ref, base, c, edge_add, face_add):
    fields, width = ref.shape[0], ref.shape[2]
    side = info[1] * (DEPTH - 1)
    lane = lanes()
    ends = (lane == 0) | (lane == width - 1)
    start = base + c * (LAYERS * 16)
    back = lax.rem(width - 2 * LAYERS * (DEPTH // LAYERS - 1 - c), width)

    def one(f, _):
        for h in range(2):
            turned = pltpu.roll(edge_add[pl.ds(pl.multiple_of(f * 16 + 8 * h, 8), 8), :], back, 1)
            for j in range(LAYERS):
                rows = pl.ds(pl.multiple_of(start + 16 * j + 8 * h, 8), 8)
                here = pltpu.roll(turned, width - 1 - 2 * (LAYERS - 1 - j), 1)
                ref[f, rows, :] = ref[f, rows, :] + jnp.where(ends, here, 0.0)
        return 0

    lax.fori_loop(0, fields, one, 0, unroll=True)

    @pl.when(side // LAYERS == c)
    def _():
        rows = pl.ds(pl.multiple_of(base + side * 16, 16), 16)
        for f in range(fields):
            ref[f, rows, :] = ref[f, rows, :] + face_add[16 * f : 16 * f + 16, :]


def pack_kernel(info, s_hbm, packet, low, high, units, s_ref, sem):
    fields, rows, width = s_ref.shape
    copies = [pltpu.make_async_copy(s_hbm.at[f], s_ref.at[f], sem.at[f]) for f in range(fields)]
    for copy in copies:
        copy.start()
    depth = rows // 16
    pair = lanes() >> 1
    start = info[1] * (rows - 16)

    def one(f, _):
        pltpu.make_async_copy(s_hbm.at[f], s_ref.at[f], sem.at[f]).wait()
        row = pl.multiple_of(f * 16, 16)
        packet[pl.ds(row, 16), :] = s_ref[f, pl.ds(pl.multiple_of(start, 16), 16), :]
        for h in range(2):
            held = jnp.zeros((8, width), jnp.float32)
            for a in range(depth):
                at = a * 16 + h * 8
                p = depth - 1 - a
                held = jnp.where(pair == p, pltpu.roll(s_ref[f, at : at + 8, :], 2 * p + 1, 1), held)
            units[pl.ds(row + 8 * h, 8), :] = held
        low[f] = s_ref[f, pl.ds(0, depth, stride=16), :]
        high[f] = s_ref[f, pl.ds(15, depth, stride=16), :]
        return 0

    lax.fori_loop(0, fields, one, 0)
    for i, value in enumerate(tighten([unit(units, u) for u in range(UNITS)])):
        packet[EDGE + 8 * i : EDGE + 8 * i + 8, :] = value


def pack(info, cells):
    fields, rows, width = cells.shape
    row = struct(fields, rows // 16, width)
    return pl.pallas_call(
        pack_kernel,
        out_shape=(struct(EDGE + 8 * TIGHT, width), row, row),
        in_specs=[SMEM, ANY],
        out_specs=(VMEM, VMEM, VMEM),
        scratch_shapes=[
            pltpu.VMEM((EDGE, width), jnp.float32),
            pltpu.VMEM(cells.shape, jnp.float32),
            pltpu.SemaphoreType.DMA((fields,)),
        ],
        compiler_params=params(48),
        name="pack",
    )(info, cells)


def relay_kernel(info, partner, ids_ref, shares_ref, *refs):
    packets, outs, (table, held) = refs[:8], refs[8:12], refs[12:]
    height, width = packets[0].shape
    own = info[0]
    lane = lanes()
    turn = lax.broadcasted_iota(jnp.int32, (8, width), 0)
    tile = ((lane >> 4) - turn) & 7
    even = (lane & 1) == 0
    held[...] = jnp.zeros_like(held)
    for q, bits in enumerate(SOURCES):
        source = own ^ bits
        other = (is_rotor(source) != is_rotor(own)).astype(jnp.int32)
        there = tile + source * 8
        for i in range(2):
            dest = own ^ (2 * (1 - other) + 4 * i)
            wanted, share = ids_ref[dest], shares_ref[dest]
            total = jnp.zeros((8, width), jnp.float32)
            for k in range(4):
                total = total + jnp.where(wanted[k : k + 1] == there, share[k : k + 1], 0.0)
            table[q, i] = total
    for q, bits in enumerate(SOURCES):
        source = own ^ bits
        other = (is_rotor(source) != is_rotor(own)).astype(jnp.int32)
        totals = [[jnp.zeros((8, width), jnp.float32)] * UNITS for _ in range(2)]
        for t in range(8):
            weights = [jnp.broadcast_to(table[q, i, t : t + 1, :], (8, width)) for i in range(2)]
            for u in range(UNITS):
                face = unit(packets[q], u)
                turned = face if t == 0 else pltpu.roll(face, 16 * t, 1)
                for i in range(2):
                    totals[i][u] = totals[i][u] + turned * weights[i]
        for i in range(2):
            for u in range(UNITS):
                rows = slice(8 * u, 8 * u + 8)
                held[1 - other, i, rows, :] = held[1 - other, i, rows, :] + totals[i][u]
        for i in range(2):
            dest = own ^ (2 * other + 4 * i)
            above = (partner[dest] == source).astype(jnp.float32)
            below = (partner[source] == dest).astype(jnp.float32)
            mask = jnp.where(even, below, above)
            for u in range(UNITS, UNITS + TIGHT):
                rows = slice(8 * u, 8 * u + 8)
                held[other, i, rows, :] = held[other, i, rows, :] + mask * unit(packets[q], u)
    for d in range(4):
        outs[d][0:EDGE, :] = held[d & 1, d >> 1, 0:EDGE, :]
        for u in range(UNITS, UNITS + TIGHT):
            rows = slice(8 * u, 8 * u + 8)
            edge = held[d & 1, d >> 1, rows, :]
            outs[d][rows, :] = jnp.where(even, pltpu.roll(edge, width - 1, 1), pltpu.roll(edge, 1, 1))


def relay(info, partner, ids, shares, packets):
    return pl.pallas_call(
        relay_kernel,
        out_shape=(struct(*packets[0].shape),) * 4,
        in_specs=[SMEM, SMEM] + [VMEM] * 10,
        out_specs=(VMEM,) * 4,
        scratch_shapes=[
            pltpu.VMEM((8, 2, 8, 128), jnp.float32),
            pltpu.VMEM((2, 2) + packets[0].shape, jnp.float32),
        ],
        compiler_params=params(48),
        name="relay",
    )(info, partner, ids, shares, *packets)


def interior_kernel(first, *refs):
    if first:
        info, coupling, v_hbm, prior, older, axial, pitch, visc, inflow, halo_low, halo_high, _ = refs[:12]
        (out, base, face, edges, edge_coef, face_coef, low, high) = refs[12:20]
        line, sem, ends = refs[20:]
    else:
        (info, coupling, v_hbm, base, axial, pitch, visc, inflow, halo_low, halo_high, _) = refs[:11]
        edge_add, face_add, out, line, sem = refs[11:]
    fields, rows, width = line.shape[0], line.shape[1] - 32, line.shape[2]
    depth = rows // 16
    step = pl.program_id(0)
    rotor = info[1] == 1
    side = info[1] * (depth - 1)

    chunks = depth // LAYERS

    def ready(c):
        chunk_copy(v_hbm, line, sem, c, 16).wait()
        if not first:
            add_terms(info, line, 16, c, edge_add, face_add)

        @pl.when(c == chunks - 1)
        def _():
            for f in range(fields):
                last = line[f, rows : rows + 16, :]
                line[f, rows + 16 : rows + 32, :] = jnp.where(rotor, 0.0, last)

    @pl.when(step == 0)
    def _():
        for c in range(chunks):
            chunk_copy(v_hbm, line, sem, c, 16).start()
        if first:
            edges[...] = jnp.zeros_like(edges)
            edge_coef[...] = jnp.zeros_like(edge_coef)
        for f in range(fields):
            line[f, 0:16, :] = jnp.where(rotor, inflow[f], 0.0)
        ready(0)

    @pl.when(step < chunks - 1)
    def _():
        ready(step + 1)

    lane = lanes()
    pair = lane >> 1
    sub = lax.broadcasted_iota(jnp.int32, (8, width), 0)
    head, tail = lane == 0, lane == width - 1
    top, bottom = sub == 0, sub == 7

    def one(j, _):
        a = step * LAYERS + j
        here = (a + 1) * 16
        coefs = []
        for h in range(2):
            speed = axial[j, 8 * h : 8 * h + 8, :]
            cross = pitch[j, 8 * h : 8 * h + 8, :]
            nu = visc[j, 8 * h : 8 * h + 8, :]
            dt = CFL / (speed + jnp.abs(cross) + 6.0 * nu + 1.5 / STEP_DT)
            even = dt * nu
            half_axial = 0.5 * dt * speed
            half_pitch = 0.5 * dt * cross
            forward, backward = even - half_axial, even + half_axial
            right, left = even - half_pitch, even + half_pitch
            centre = -(1.5 / STEP_DT) * dt - 6.0 * even
            if first:
                ends[j, 8 * h : 8 * h + 8, :] = jnp.where(tail, right, left)
            right, left = jnp.where(tail, 0.0, right), jnp.where(head, 0.0, left)
            coefs.append((dt, centre, forward, backward, right, left, even))

        def at(f, h, shift=0):
            return line[f, pl.ds(pl.multiple_of(here + 16 * shift + 8 * h, 8), 8), :]

        values = [[at(f, h) for h in range(2)] for f in range(fields)]
        for f in range(fields):
            x0, x1 = values[f]
            r0, r1 = pltpu.roll(x0, 1, 0), pltpu.roll(x1, 1, 0)
            d0, d1 = pltpu.roll(x0, 7, 0), pltpu.roll(x1, 7, 0)
            before = (jnp.where(top, halo_low[f, pl.ds(a, 1), :], r0), jnp.where(top, r0, r1))
            after = (jnp.where(bottom, d1, d0), jnp.where(bottom, halo_high[f, pl.ds(a, 1), :], d1))
            for h in range(2):
                dt, centre, forward, backward, right, left, even = coefs[h]
                x = values[f][h]
                mixed = coupling[f, 0] * values[0][h]
                for g in range(1, fields):
                    mixed = mixed + coupling[f, g] * values[g][h]
                change = (
                    (centre * x + even * (before[h] + after[h]))
                    + (forward * at(f, h, 1) + backward * at(f, h, -1))
                    + (right * pltpu.roll(x, width - 1, 1) + left * pltpu.roll(x, 1, 1))
                    - dt * mixed
                )
                place = (f, j, slice(8 * h, 8 * h + 8))
                if first:
                    known = dt * (prior[place] - 0.25 * older[place])
                    base[place] = known
                    moved = x + 0.5 * (known + change)
                    out[place] = moved
                    if h == 0:
                        low[f, pl.ds(j, 1), :] = moved[0:1]
                    else:
                        high[f, pl.ds(j, 1), :] = moved[7:8]
                else:
                    out[place] = x + (base[place] + change)
        return 0

    lax.fori_loop(0, LAYERS, one, 0, unroll=4)

    if first:

        def gather(target, rows, layer):
            part = jnp.zeros((8, width), jnp.float32)
            for j in range(LAYERS):
                p = LAYERS - 1 - j
                part = jnp.where(pair == p, pltpu.roll(layer(j), 2 * p + 1, 1), part)
            place = chunks - 1 - step
            part = pltpu.roll(part, 2 * LAYERS * place, 1)
            target[rows, :] = jnp.where(pair // LAYERS == place, part, target[rows, :])

        for h in range(2):
            rows_h = slice(8 * h, 8 * h + 8)
            gather(edge_coef, rows_h, lambda j: ends[j, rows_h, :])
            for f in range(fields):
                spot = slice(16 * f + 8 * h, 16 * f + 8 * h + 8)
                gather(edges, spot, lambda j: out[f, j, rows_h, :])

        @pl.when(step == side // LAYERS)
        def _():
            j = lax.rem(side, LAYERS)
            dt = CFL / (axial[j] + jnp.abs(pitch[j]) + 6.0 * visc[j] + 1.5 / STEP_DT)
            drift = 0.5 * axial[j]
            face_coef[...] = dt * (visc[j] + jnp.where(rotor, -drift, drift))
            for f in range(fields):
                face[16 * f : 16 * f + 16, :] = out[f, j]


def interior(first, info, coupling, v, given, speeds, inflow, halos, order, adds=()):
    fields, rows, width = v.shape
    depth = rows // 16
    whole = struct(fields, depth, 16, width)
    block = pl.BlockSpec((fields, LAYERS, 16, width), lambda i: (0, i, 0, 0))
    cell = pl.BlockSpec((LAYERS, 16, width), lambda i: (i, 0, 0))
    halo = fixed(*halos[0].shape)
    out_shape, out_specs = [whole], [block]
    if first:
        small = [(EDGE, width), (EDGE, width), (16, width), (16, width)]
        out_shape += [whole] + [struct(*s) for s in small]
        out_specs += [block] + [fixed(*s) for s in small]
        out_shape += [struct(fields, depth, width)] * 2
        out_specs += [pl.BlockSpec((fields, LAYERS, width), lambda i: (0, i, 0))] * 2
    return pl.pallas_call(
        functools.partial(interior_kernel, first),
        grid=(depth // LAYERS,),
        out_shape=out_shape,
        in_specs=[SMEM, SMEM, ANY]
        + [block] * len(given)
        + [cell] * 3
        + [fixed(*inflow.shape), halo, halo, ANY]
        + [fixed(*a.shape) for a in adds],
        out_specs=out_specs,
        scratch_shapes=[
            pltpu.VMEM((fields, rows + 32, width), jnp.float32),
            pltpu.SemaphoreType.DMA((depth // LAYERS,)),
        ]
        + [pltpu.VMEM((LAYERS, 16, width), jnp.float32)] * int(first),
        compiler_params=params(48),
        cost_estimate=pl.CostEstimate(flops=30_000_000, bytes_accessed=12_000_000, transcendentals=0),
        name="first_interior" if first else "second_interior",
    )(info, coupling, v, *given, *speeds, inflow, *halos, order, *adds)


def terms(scale, parts, edge_coef, face_coef):
    ghosts = loosen([summed(parts, UNITS + i) for i in range(TIGHT)])
    edge_terms = [scale * edge_coef[8 * (u & 1) : 8 * (u & 1) + 8, :] * ghosts[u] for u in range(UNITS)]
    face_terms = [
        scale * face_coef[8 * (u & 1) : 8 * (u & 1) + 8, :] * summed(parts, u) for u in range(UNITS)
    ]
    return edge_terms, face_terms


def boundary_kernel(info, *refs):
    parts, (face, edges, edge_coef, face_coef, low, high) = refs[:4], refs[4:10]
    packet, edge_add, face_add, new_low, new_high = refs[10:]
    width = face.shape[1]
    side = info[1] * (DEPTH - 1)
    lane = lanes()
    ends = (lane == 0) | (lane == width - 1)
    spot = DEPTH - 1 - side
    here = (lane >> 1) == spot
    layer = lax.broadcasted_iota(jnp.int32, (8, width), 0)
    edge_terms, face_terms = terms(0.5, parts, edge_coef, face_coef)
    packed = []
    for u in range(UNITS):
        rows = slice(8 * u, 8 * u + 8)
        edge_add[rows, :] = edge_terms[u]
        face_add[rows, :] = face_terms[u]
        turned = pltpu.roll(edge_terms[u], width - 1 - 2 * spot, 1)
        packet[rows, :] = unit(face, u) + face_terms[u] + jnp.where(ends, turned, 0.0)
        turned = pltpu.roll(face_terms[u], 2 * spot + 1, 1)
        packed.append(unit(edges, u) + edge_terms[u] + jnp.where(here, turned, 0.0))
    for i, value in enumerate(tighten(packed)):
        packet[EDGE + 8 * i : EDGE + 8 * i + 8, :] = value
    for old, new, last in ((low, new_low, 0), (high, new_high, 1)):
        row = 7 * last
        for f in range(UNITS // 2):
            edge = jnp.broadcast_to(edge_terms[2 * f + last][row : row + 1], (8, width))
            slid = jnp.broadcast_to(face_terms[2 * f + last][row : row + 1], (8, width))
            for a in range(0, DEPTH, 8):
                turned = pltpu.roll(edge, width + 1 - 2 * (DEPTH - a), 1, stride=2, stride_axis=0)
                added = jnp.where(ends, turned, 0.0) + jnp.where(layer + a == side, slid, 0.0)
                new[f, a : a + 8, :] = old[f, a : a + 8, :] + added


def boundary(info, parts, face, edges, edge_coef, face_coef, low, high):
    small, line = struct(*face.shape), struct(*low.shape)
    return pl.pallas_call(
        boundary_kernel,
        out_shape=(struct(*parts[0].shape), small, small, line, line),
        in_specs=[SMEM] + [VMEM] * 10,
        out_specs=(VMEM,) * 5,
        compiler_params=params(48),
        name="boundary",
    )(info, *parts, face, edges, edge_coef, face_coef, low, high)


def final_kernel(info, v, *refs):
    parts, (edge_coef, face_coef, out, held, edge_add, face_add, arrived, left) = refs[:4], refs[4:]
    chunks = DEPTH // LAYERS
    for c in range(chunks):
        chunk_copy(v, held, arrived, c).start()
    edge_terms, face_terms = terms(1.0, parts, edge_coef, face_coef)
    for u in range(UNITS):
        edge_add[8 * u : 8 * u + 8, :] = edge_terms[u]
        face_add[8 * u : 8 * u + 8, :] = face_terms[u]

    def one(c, _):
        chunk_copy(v, held, arrived, c).wait()
        add_terms(info, held, 0, c, edge_add, face_add)
        chunk_copy(held, out, left, c).start()
        return 0

    lax.fori_loop(0, chunks, one, 0)
    for c in range(chunks):
        chunk_copy(held, out, left, c).wait()


def correct_final(info, v, parts, edge_coef, face_coef):
    width = v.shape[2]
    return pl.pallas_call(
        final_kernel,
        out_shape=struct(*v.shape),
        in_specs=[SMEM, ANY] + [VMEM] * 6,
        out_specs=ANY,
        scratch_shapes=[pltpu.VMEM(v.shape, jnp.float32)]
        + [pltpu.VMEM((EDGE, width), jnp.float32)] * 2
        + [pltpu.SemaphoreType.DMA((DEPTH // LAYERS,))] * 2,
        compiler_params=params(48),
        name="correct_final",
    )(info, v, *parts, edge_coef, face_coef)


def flip(value, bits):
    return lax.ppermute(value, "passage", [(i, i ^ bits) for i in range(lax.axis_size("passage"))])


def span_halos(low, high):
    count = lax.axis_size("span")
    up = [(i, i + 1) for i in range(count - 1)]
    down = [(i + 1, i) for i in range(count - 1)]
    return lax.ppermute(high, "span", up), lax.ppermute(low, "span", down)


def on_device(
    state,
    previous,
    earlier,
    axial_speed,
    pitch_speed,
    viscosity,
    inflow,
    coupling,
    partner,
    tile_ids,
    tile_weights,
):
    own = lax.axis_index("passage")
    half = lax.axis_size("passage") // 2
    rotor = (own + (own >= half).astype(jnp.int32)) % 4 < 2
    info = jnp.stack([own, rotor.astype(jnp.int32)])
    fields, _, depth, spans, width = state.shape
    cells = state.reshape(fields, depth * spans, width)
    speeds = (axial_speed[0], pitch_speed[0], viscosity[0])
    weights = tile_weights.astype(jnp.float32)
    shares = weights / jnp.sum(weights, axis=2, keepdims=True)
    cut = width // tile_ids.shape[1]
    wide_ids = jnp.repeat(jnp.swapaxes(tile_ids, 1, 2), cut, axis=2)
    wide_shares = jnp.repeat(jnp.swapaxes(shares, 1, 2), cut, axis=2)

    def exchange(packet):
        near = [packet] + [flip(packet, k) for k in X_FLIPS]
        far = [flip(p, CORE_FLIP) for p in near]
        sent = relay(info, partner, wide_ids, wide_shares, near + far)
        return [sent[0]] + [flip(p, k) for p, k in zip(sent[1:], Z_FLIPS)]

    packet, low, high = pack(info, cells)
    parts = exchange(packet)
    halos = span_halos(low, high)
    middle, base, face, edges, edge_coef, face_coef, low, high = interior(
        True, info, coupling, cells, (previous[:, 0], earlier[:, 0]), speeds, inflow, halos, parts[0]
    )
    packet, edge_add, face_add, low, high = boundary(
        info, parts, face, edges, edge_coef, face_coef, low, high
    )
    halos = span_halos(low, high)
    parts = exchange(packet)
    (updated,) = interior(
        False,
        info,
        coupling,
        middle.reshape(cells.shape),
        (base,),
        speeds,
        inflow,
        halos,
        parts[0],
        (edge_add, face_add),
    )
    updated = correct_final(info, updated.reshape(cells.shape), parts, edge_coef, face_coef)
    return updated.reshape(state.shape)


def solution(mesh):
    placed = (
        P(None, "passage", None, "span", None),
        P(None, "passage", None, "span", None),
        P(None, "passage", None, "span", None),
        P("passage", None, "span", None),
        P("passage", None, "span", None),
        P("passage", None, "span", None),
        P(None, "span", None),
        P(),
        P(),
        P(),
        P(),
    )
    return jax.shard_map(
        on_device,
        mesh=mesh,
        in_specs=placed,
        out_specs=P(None, "passage", None, "span", None),
        check_vma=False,
    )
```

```python
import functools

import jax
import jax.numpy as jnp
from jax import lax
from jax.experimental import pallas as pl
from jax.experimental.pallas import tpu as pltpu
from jax.sharding import PartitionSpec as P

CFL = 0.8
STEP_DT = 2.0

X_FLIPS = (8, 16, 24)
Z_FLIPS = (2, 4, 6)
CORE_FLIP = 1
SOURCES = (0, 8, 16, 24, 1, 9, 17, 25)

LAYERS = 8
UNITS = 14
EDGE = UNITS * 8
DEPTH = 48
TIGHT = 11

SMEM = pl.BlockSpec(memory_space=pltpu.SMEM)
VMEM = pl.BlockSpec(memory_space=pltpu.VMEM)
ANY = pl.BlockSpec(memory_space=pl.ANY)


def params(mib):
    return pltpu.CompilerParams(vmem_limit_bytes=mib * 1024 * 1024)


def lanes(shape=(8, 128)):
    return lax.broadcasted_iota(jnp.int32, shape, len(shape) - 1)


def struct(*shape):
    return jax.ShapeDtypeStruct(shape, jnp.float32)


def fixed(*shape):
    return pl.BlockSpec(shape, lambda i: (0,) * len(shape))


def unit(ref, u):
    return ref[8 * u : 8 * u + 8, :]


def tighten(units):
    lane = lanes()
    packed = []
    for first in range(0, 12, 4):
        for j in range(3):
            spare = pltpu.roll(units[first + 3], 96 - 32 * j, 1)
            packed.append(jnp.where(lane < 96, units[first + j], spare))
    return packed + list(units[12:])


def loosen(packed):
    lane = lanes()
    units = []
    for first in range(0, 9, 3):
        a, b, c = packed[first : first + 3]
        last = jnp.where(
            lane < 32,
            pltpu.roll(a, 32, 1),
            jnp.where(lane < 64, pltpu.roll(b, 64, 1), pltpu.roll(c, 96, 1)),
        )
        units += [a, b, c, last]
    return units + list(packed[9:])


def is_rotor(passage):
    return ((passage + (passage >= 16).astype(jnp.int32)) & 3) < 2


def summed(parts, u):
    return (unit(parts[0], u) + unit(parts[1], u)) + (unit(parts[2], u) + unit(parts[3], u))


def chunk_copy(source, target, sem, c, base=0):
    rows = LAYERS * 16
    here = pl.multiple_of(c * rows, rows)
    there = pl.multiple_of(here + base, 16)
    return pltpu.make_async_copy(
        source.at[:, pl.ds(here, rows), :], target.at[:, pl.ds(there, rows), :], sem.at[c]
    )


def add_terms(info, old, ref, base, c, edge_add, face_add):
    fields, width = ref.shape[0], ref.shape[2]
    side = info[1] * (DEPTH - 1)
    lane = lanes()
    ends = (lane == 0) | (lane == width - 1)
    start = base + c * (LAYERS * 16)
    back = lax.rem(width - 2 * LAYERS * (DEPTH // LAYERS - 1 - c), width)

    def one(f, _):
        for h in range(2):
            turned = pltpu.roll(edge_add[pl.ds(pl.multiple_of(f * 16 + 8 * h, 8), 8), :], back, 1)
            for j in range(LAYERS):
                rows = pl.ds(pl.multiple_of(start + 16 * j + 8 * h, 8), 8)
                here = pltpu.roll(turned, width - 1 - 2 * (LAYERS - 1 - j), 1)
                ref[f, rows, :] = old[f, rows, :] + jnp.where(ends, here, 0.0)
        return 0

    lax.fori_loop(0, fields, one, 0, unroll=True)

    @pl.when(side // LAYERS == c)
    def _():
        rows = pl.ds(pl.multiple_of(base + side * 16, 16), 16)
        for f in range(fields):
            ref[f, rows, :] = ref[f, rows, :] + face_add[16 * f : 16 * f + 16, :]


def pack_kernel(info, s_ref, packet, low, high, units):
    fields, rows, width = s_ref.shape
    depth = rows // 16
    pair = lanes() >> 1
    start = info[1] * (rows - 16)

    def one(f, _):
        row = pl.multiple_of(f * 16, 16)
        packet[pl.ds(row, 16), :] = s_ref[f, pl.ds(pl.multiple_of(start, 16), 16), :]
        for h in range(2):
            held = jnp.zeros((8, width), jnp.float32)
            for a in range(depth):
                at = a * 16 + h * 8
                p = depth - 1 - a
                held = jnp.where(pair == p, pltpu.roll(s_ref[f, at : at + 8, :], 2 * p + 1, 1), held)
            units[pl.ds(row + 8 * h, 8), :] = held
        low[f] = s_ref[f, pl.ds(0, depth, stride=16), :]
        high[f] = s_ref[f, pl.ds(15, depth, stride=16), :]
        return 0

    lax.fori_loop(0, fields, one, 0)
    for i, value in enumerate(tighten([unit(units, u) for u in range(UNITS)])):
        packet[EDGE + 8 * i : EDGE + 8 * i + 8, :] = value


def pack(info, cells):
    fields, rows, width = cells.shape
    row = struct(fields, rows // 16, width)
    return pl.pallas_call(
        pack_kernel,
        out_shape=(struct(EDGE + 8 * TIGHT, width), row, row),
        in_specs=[SMEM, VMEM],
        out_specs=(VMEM, VMEM, VMEM),
        scratch_shapes=[pltpu.VMEM((EDGE, width), jnp.float32)],
        compiler_params=params(48),
        name="pack",
    )(info, cells)


def relay_kernel(info, partner, ids_ref, shares_ref, *refs):
    packets, outs, (table, held) = refs[:8], refs[8:12], refs[12:]
    height, width = packets[0].shape
    own = info[0]
    lane = lanes()
    turn = lax.broadcasted_iota(jnp.int32, (8, width), 0)
    tile = ((lane >> 4) - turn) & 7
    even = (lane & 1) == 0
    held[...] = jnp.zeros_like(held)
    for q, bits in enumerate(SOURCES):
        source = own ^ bits
        other = (is_rotor(source) != is_rotor(own)).astype(jnp.int32)
        there = tile + source * 8
        for i in range(2):
            dest = own ^ (2 * (1 - other) + 4 * i)
            wanted, share = ids_ref[dest], shares_ref[dest]
            total = jnp.zeros((8, width), jnp.float32)
            for k in range(4):
                total = total + jnp.where(wanted[k : k + 1] == there, share[k : k + 1], 0.0)
            table[q, i] = total
    for q, bits in enumerate(SOURCES):
        source = own ^ bits
        other = (is_rotor(source) != is_rotor(own)).astype(jnp.int32)
        totals = [[jnp.zeros((8, width), jnp.float32)] * UNITS for _ in range(2)]
        for t in range(8):
            weights = [jnp.broadcast_to(table[q, i, t : t + 1, :], (8, width)) for i in range(2)]
            for u in range(UNITS):
                face = unit(packets[q], u)
                turned = face if t == 0 else pltpu.roll(face, 16 * t, 1)
                for i in range(2):
                    totals[i][u] = totals[i][u] + turned * weights[i]
        for i in range(2):
            for u in range(UNITS):
                rows = slice(8 * u, 8 * u + 8)
                held[1 - other, i, rows, :] = held[1 - other, i, rows, :] + totals[i][u]
        for i in range(2):
            dest = own ^ (2 * other + 4 * i)
            above = (partner[dest] == source).astype(jnp.float32)
            below = (partner[source] == dest).astype(jnp.float32)
            mask = jnp.where(even, below, above)
            for u in range(UNITS, UNITS + TIGHT):
                rows = slice(8 * u, 8 * u + 8)
                held[other, i, rows, :] = held[other, i, rows, :] + mask * unit(packets[q], u)
    for d in range(4):
        outs[d][0:EDGE, :] = held[d & 1, d >> 1, 0:EDGE, :]
        for u in range(UNITS, UNITS + TIGHT):
            rows = slice(8 * u, 8 * u + 8)
            edge = held[d & 1, d >> 1, rows, :]
            outs[d][rows, :] = jnp.where(even, pltpu.roll(edge, width - 1, 1), pltpu.roll(edge, 1, 1))


def relay(info, partner, ids, shares, packets):
    return pl.pallas_call(
        relay_kernel,
        out_shape=(struct(*packets[0].shape),) * 4,
        in_specs=[SMEM, SMEM] + [VMEM] * 10,
        out_specs=(VMEM,) * 4,
        scratch_shapes=[
            pltpu.VMEM((8, 2, 8, 128), jnp.float32),
            pltpu.VMEM((2, 2) + packets[0].shape, jnp.float32),
        ],
        compiler_params=params(48),
        name="relay",
    )(info, partner, ids, shares, *packets)


def interior_kernel(first, *refs):
    if first:
        info, coupling, v_hbm, prior, older, axial, pitch, visc, inflow, halo_low, halo_high, _ = refs[:12]
        (out, face, edges, edge_coef, face_coef, low, high) = refs[12:19]
        line, sem, ends = refs[19:]
    else:
        info, coupling, v_hbm, prior, older, axial, pitch, visc, inflow, halo_low, halo_high, _ = refs[:12]
        edge_add, face_add, out, line, sem = refs[12:]
    fields, rows, width = line.shape[0], line.shape[1] - 32, line.shape[2]
    depth = rows // 16
    step = pl.program_id(0)
    rotor = info[1] == 1
    side = info[1] * (depth - 1)

    chunks = depth // LAYERS

    def ready(c):
        chunk_copy(v_hbm, line, sem, c, 16).wait()
        if not first:
            add_terms(info, line, line, 16, c, edge_add, face_add)

        @pl.when(c == chunks - 1)
        def _():
            for f in range(fields):
                last = line[f, rows : rows + 16, :]
                line[f, rows + 16 : rows + 32, :] = jnp.where(rotor, 0.0, last)

    @pl.when(step == 0)
    def _():
        for c in range(chunks):
            chunk_copy(v_hbm, line, sem, c, 16).start()
        if first:
            edges[...] = jnp.zeros_like(edges)
            edge_coef[...] = jnp.zeros_like(edge_coef)
        for f in range(fields):
            line[f, 0:16, :] = jnp.where(rotor, inflow[f], 0.0)
        ready(0)

    @pl.when(step < chunks - 1)
    def _():
        ready(step + 1)

    lane = lanes()
    pair = lane >> 1
    sub = lax.broadcasted_iota(jnp.int32, (8, width), 0)
    head, tail = lane == 0, lane == width - 1
    top, bottom = sub == 0, sub == 7

    def one(j, _):
        a = step * LAYERS + j
        here = (a + 1) * 16
        coefs = []
        for h in range(2):
            speed = axial[j, 8 * h : 8 * h + 8, :]
            cross = pitch[j, 8 * h : 8 * h + 8, :]
            nu = visc[j, 8 * h : 8 * h + 8, :]
            dt = CFL / (speed + jnp.abs(cross) + 6.0 * nu + 1.5 / STEP_DT)
            even = dt * nu
            half_axial = 0.5 * dt * speed
            half_pitch = 0.5 * dt * cross
            forward, backward = even - half_axial, even + half_axial
            right, left = even - half_pitch, even + half_pitch
            centre = -(1.5 / STEP_DT) * dt - 6.0 * even
            if first:
                ends[j, 8 * h : 8 * h + 8, :] = jnp.where(tail, right, left)
            right, left = jnp.where(tail, 0.0, right), jnp.where(head, 0.0, left)
            coefs.append((dt, centre, forward, backward, right, left, even))

        def at(f, h, shift=0):
            return line[f, pl.ds(pl.multiple_of(here + 16 * shift + 8 * h, 8), 8), :]

        values = [[at(f, h) for h in range(2)] for f in range(fields)]
        for f in range(fields):
            x0, x1 = values[f]
            r0, r1 = pltpu.roll(x0, 1, 0), pltpu.roll(x1, 1, 0)
            d0, d1 = pltpu.roll(x0, 7, 0), pltpu.roll(x1, 7, 0)
            before = (jnp.where(top, halo_low[f, pl.ds(a, 1), :], r0), jnp.where(top, r0, r1))
            after = (jnp.where(bottom, d1, d0), jnp.where(bottom, halo_high[f, pl.ds(a, 1), :], d1))
            for h in range(2):
                dt, centre, forward, backward, right, left, even = coefs[h]
                x = values[f][h]
                mixed = coupling[f, 0] * values[0][h]
                for g in range(1, fields):
                    mixed = mixed + coupling[f, g] * values[g][h]
                change = (
                    (centre * x + even * (before[h] + after[h]))
                    + (forward * at(f, h, 1) + backward * at(f, h, -1))
                    + (right * pltpu.roll(x, width - 1, 1) + left * pltpu.roll(x, 1, 1))
                    - dt * mixed
                )
                place = (f, j, slice(8 * h, 8 * h + 8))
                change = change + dt * (prior[place] - 0.25 * older[place])
                if first:
                    moved = x + 0.5 * change
                    out[place] = moved
                    if h == 0:
                        low[f, pl.ds(j, 1), :] = moved[0:1]
                    else:
                        high[f, pl.ds(j, 1), :] = moved[7:8]
                else:
                    out[place] = x + change
        return 0

    lax.fori_loop(0, LAYERS, one, 0, unroll=4)

    if first:

        def gather(target, rows, layer):
            part = jnp.zeros((8, width), jnp.float32)
            for j in range(LAYERS):
                p = LAYERS - 1 - j
                part = jnp.where(pair == p, pltpu.roll(layer(j), 2 * p + 1, 1), part)
            place = chunks - 1 - step
            part = pltpu.roll(part, 2 * LAYERS * place, 1)
            target[rows, :] = jnp.where(pair // LAYERS == place, part, target[rows, :])

        for h in range(2):
            rows_h = slice(8 * h, 8 * h + 8)
            gather(edge_coef, rows_h, lambda j: ends[j, rows_h, :])
            for f in range(fields):
                spot = slice(16 * f + 8 * h, 16 * f + 8 * h + 8)
                gather(edges, spot, lambda j: out[f, j, rows_h, :])

        @pl.when(step == side // LAYERS)
        def _():
            j = lax.rem(side, LAYERS)
            dt = CFL / (axial[j] + jnp.abs(pitch[j]) + 6.0 * visc[j] + 1.5 / STEP_DT)
            drift = 0.5 * axial[j]
            face_coef[...] = dt * (visc[j] + jnp.where(rotor, -drift, drift))
            for f in range(fields):
                face[16 * f : 16 * f + 16, :] = out[f, j]


def interior(first, info, coupling, v, given, speeds, inflow, halos, order, adds=()):
    fields, rows, width = v.shape
    depth = rows // 16
    whole = struct(fields, depth, 16, width)
    block = pl.BlockSpec((fields, LAYERS, 16, width), lambda i: (0, i, 0, 0))
    cell = pl.BlockSpec((LAYERS, 16, width), lambda i: (i, 0, 0))
    halo = fixed(*halos[0].shape)
    out_shape, out_specs = [whole], [block]
    if first:
        small = [(EDGE, width), (EDGE, width), (16, width), (16, width)]
        out_shape += [struct(*s) for s in small]
        out_specs += [fixed(*s) for s in small]
        out_shape += [struct(fields, depth, width)] * 2
        out_specs += [pl.BlockSpec((fields, LAYERS, width), lambda i: (0, i, 0))] * 2
    return pl.pallas_call(
        functools.partial(interior_kernel, first),
        grid=(depth // LAYERS,),
        out_shape=out_shape,
        in_specs=[SMEM, SMEM, ANY]
        + [block] * len(given)
        + [cell] * 3
        + [fixed(*inflow.shape), halo, halo, ANY]
        + [fixed(*a.shape) for a in adds],
        out_specs=out_specs,
        scratch_shapes=[
            pltpu.VMEM((fields, rows + 32, width), jnp.float32),
            pltpu.SemaphoreType.DMA((depth // LAYERS,)),
        ]
        + [pltpu.VMEM((LAYERS, 16, width), jnp.float32)] * int(first),
        compiler_params=params(48 if first else 42),
        cost_estimate=pl.CostEstimate(flops=30_000_000, bytes_accessed=12_000_000, transcendentals=0),
        name="first_interior" if first else "second_interior",
    )(info, coupling, v, *given, *speeds, inflow, *halos, order, *adds)


def terms(scale, parts, edge_coef, face_coef):
    ghosts = loosen([summed(parts, UNITS + i) for i in range(TIGHT)])
    edge_terms = [scale * edge_coef[8 * (u & 1) : 8 * (u & 1) + 8, :] * ghosts[u] for u in range(UNITS)]
    face_terms = [
        scale * face_coef[8 * (u & 1) : 8 * (u & 1) + 8, :] * summed(parts, u) for u in range(UNITS)
    ]
    return edge_terms, face_terms


def boundary_kernel(info, *refs):
    parts, (face, edges, edge_coef, face_coef, low, high) = refs[:4], refs[4:10]
    packet, edge_add, face_add, new_low, new_high = refs[10:]
    width = face.shape[1]
    side = info[1] * (DEPTH - 1)
    lane = lanes()
    ends = (lane == 0) | (lane == width - 1)
    spot = DEPTH - 1 - side
    here = (lane >> 1) == spot
    layer = lax.broadcasted_iota(jnp.int32, (8, width), 0)
    edge_terms, face_terms = terms(0.5, parts, edge_coef, face_coef)
    packed = []
    for u in range(UNITS):
        rows = slice(8 * u, 8 * u + 8)
        edge_add[rows, :] = edge_terms[u]
        face_add[rows, :] = face_terms[u]
        turned = pltpu.roll(edge_terms[u], width - 1 - 2 * spot, 1)
        packet[rows, :] = unit(face, u) + face_terms[u] + jnp.where(ends, turned, 0.0)
        turned = pltpu.roll(face_terms[u], 2 * spot + 1, 1)
        packed.append(unit(edges, u) + edge_terms[u] + jnp.where(here, turned, 0.0))
    for i, value in enumerate(tighten(packed)):
        packet[EDGE + 8 * i : EDGE + 8 * i + 8, :] = value
    for old, new, last in ((low, new_low, 0), (high, new_high, 1)):
        row = 7 * last
        for f in range(UNITS // 2):
            edge = jnp.broadcast_to(edge_terms[2 * f + last][row : row + 1], (8, width))
            slid = jnp.broadcast_to(face_terms[2 * f + last][row : row + 1], (8, width))
            for a in range(0, DEPTH, 8):
                turned = pltpu.roll(edge, width + 1 - 2 * (DEPTH - a), 1, stride=2, stride_axis=0)
                added = jnp.where(ends, turned, 0.0) + jnp.where(layer + a == side, slid, 0.0)
                new[f, a : a + 8, :] = old[f, a : a + 8, :] + added


def boundary(info, parts, face, edges, edge_coef, face_coef, low, high):
    small, line = struct(*face.shape), struct(*low.shape)
    return pl.pallas_call(
        boundary_kernel,
        out_shape=(struct(*parts[0].shape), small, small, line, line),
        in_specs=[SMEM] + [VMEM] * 10,
        out_specs=(VMEM,) * 5,
        compiler_params=params(48),
        name="boundary",
    )(info, *parts, face, edges, edge_coef, face_coef, low, high)


def final_kernel(info, v, *refs):
    parts, (edge_coef, face_coef, out, held, edge_add, face_add, left) = refs[:4], refs[4:]
    chunks = DEPTH // LAYERS
    edge_terms, face_terms = terms(1.0, parts, edge_coef, face_coef)
    for u in range(UNITS):
        edge_add[8 * u : 8 * u + 8, :] = edge_terms[u]
        face_add[8 * u : 8 * u + 8, :] = face_terms[u]

    def one(c, _):
        add_terms(info, v, held, 0, c, edge_add, face_add)
        chunk_copy(held, out, left, c).start()
        return 0

    lax.fori_loop(0, chunks, one, 0)
    for c in range(chunks):
        chunk_copy(held, out, left, c).wait()


def correct_final(info, v, parts, edge_coef, face_coef):
    width = v.shape[2]
    return pl.pallas_call(
        final_kernel,
        out_shape=struct(*v.shape),
        in_specs=[SMEM] + [VMEM] * 7,
        out_specs=ANY,
        scratch_shapes=[pltpu.VMEM(v.shape, jnp.float32)]
        + [pltpu.VMEM((EDGE, width), jnp.float32)] * 2
        + [pltpu.SemaphoreType.DMA((DEPTH // LAYERS,))],
        compiler_params=params(48),
        name="correct_final",
    )(info, v, *parts, edge_coef, face_coef)


def flip(value, bits):
    return lax.ppermute(value, "passage", [(i, i ^ bits) for i in range(lax.axis_size("passage"))])


def span_halos(low, high):
    count = lax.axis_size("span")
    up = [(i, i + 1) for i in range(count - 1)]
    down = [(i + 1, i) for i in range(count - 1)]
    return lax.ppermute(high, "span", up), lax.ppermute(low, "span", down)


def on_device(
    state,
    previous,
    earlier,
    axial_speed,
    pitch_speed,
    viscosity,
    inflow,
    coupling,
    partner,
    tile_ids,
    tile_weights,
):
    own = lax.axis_index("passage")
    half = lax.axis_size("passage") // 2
    rotor = (own + (own >= half).astype(jnp.int32)) % 4 < 2
    info = jnp.stack([own, rotor.astype(jnp.int32)])
    fields, _, depth, spans, width = state.shape
    cells = state.reshape(fields, depth * spans, width)
    speeds = (axial_speed[0], pitch_speed[0], viscosity[0])
    levels = (previous[:, 0], earlier[:, 0])
    weights = tile_weights.astype(jnp.float32)
    shares = weights / jnp.sum(weights, axis=2, keepdims=True)
    cut = width // tile_ids.shape[1]
    wide_ids = jnp.repeat(jnp.swapaxes(tile_ids, 1, 2), cut, axis=2)
    wide_shares = jnp.repeat(jnp.swapaxes(shares, 1, 2), cut, axis=2)

    def exchange(packet):
        near = [packet] + [flip(packet, k) for k in X_FLIPS]
        far = [flip(p, CORE_FLIP) for p in near]
        sent = relay(info, partner, wide_ids, wide_shares, near + far)
        return [sent[0]] + [flip(p, k) for p, k in zip(sent[1:], Z_FLIPS)]

    packet, low, high = pack(info, cells)
    parts = exchange(packet)
    halos = span_halos(low, high)
    middle, face, edges, edge_coef, face_coef, low, high = interior(
        True, info, coupling, cells, levels, speeds, inflow, halos, parts[0]
    )
    packet, edge_add, face_add, low, high = boundary(
        info, parts, face, edges, edge_coef, face_coef, low, high
    )
    halos = span_halos(low, high)
    parts = exchange(packet)
    (updated,) = interior(
        False,
        info,
        coupling,
        middle.reshape(cells.shape),
        levels,
        speeds,
        inflow,
        halos,
        parts[0],
        (edge_add, face_add),
    )
    updated = correct_final(info, updated.reshape(cells.shape), parts, edge_coef, face_coef)
    return updated.reshape(state.shape)


def solution(mesh):
    placed = (
        P(None, "passage", None, "span", None),
        P(None, "passage", None, "span", None),
        P(None, "passage", None, "span", None),
        P("passage", None, "span", None),
        P("passage", None, "span", None),
        P("passage", None, "span", None),
        P(None, "span", None),
        P(),
        P(),
        P(),
        P(),
    )
    return jax.shard_map(
        on_device,
        mesh=mesh,
        in_specs=placed,
        out_specs=P(None, "passage", None, "span", None),
        check_vma=False,
    )
```
